32 devices in a mesh: space: 8 (over z, y), chaos: 4 (over x, core).
Axes of the slice: x: 2, y: 2, z: 4, core: 2. Of those that a mesh axis runs over, the one named last changes fastest.
Arguments:
- load_vectors: bfloat16 [256, 2, 16, 3072], P('chaos', None, None, 'space'), may hold values from -6 to 6
- stiff_tiles: bfloat16 [32, 3, 8, 2, 96, 96], P('space'), may hold values from -0.09375 to 0.09375
- tile_columns: int32 [32, 3], P('space'), may hold values from 0 to 5, as said below
- chaos_index: int32 [8, 256, 32], replicated, may hold values from 0 to 255, as said below
- chaos_value: bfloat16 [8, 256, 32], replicated, may hold values from -1 to 1
Outputs:
- response: float32 [256, 2, 16, 3072], P('chaos', None, None, 'space')
The draws below stay inside these ranges and needn't reach their ends.
Inputs may be any that keep to these rules, and one draw needn't show every extreme that they name: `tile_columns`: in row b of one subdomain with local index l = b % 4, the three numbers are l + 1, one of 0 to l, and one of l + 2 to 5. `chaos_index`: for every k and i the 32 numbers are distinct and the first is i.
All inputs are finite; a program needn't handle non-finite values.
Results may differ from the reference program's by a relative error of at most 0.0029.
Values may be sent and summed in bfloat16 or wider, within the bound.
No kernel may reach another device: no remote copies, remote signals or barrier semaphores. Data moves between devices by JAX's collectives and lax.ppermute only.
A program may use at most 128 MiB of HBM per device.

```python
import jax
import jax.numpy as jnp
from jax import lax

TILE = 96
NKL = 8
P_SIZE = 256
NZC = 32
NNZ = 3
BLK_DEV = 4
LOADS = 16
NBLK = 32
NDOF = 3072


def draw_tile_columns(key, part):
    left_key = jax.random.fold_in(key, 11)
    right_key = jax.random.fold_in(key, 12)
    local_row = jnp.arange(NBLK, dtype=jnp.int32) % BLK_DEV
    diagonal = local_row + 1
    left_raw = jax.random.randint(left_key, (NBLK,), 0, 1 << 20, dtype=jnp.int32)
    right_raw = jax.random.randint(right_key, (NBLK,), 0, 1 << 20, dtype=jnp.int32)
    left_col = left_raw % (local_row + 1)
    right_col = local_row + 2 + right_raw % (BLK_DEV - local_row)
    return jnp.stack([diagonal, left_col, right_col], axis=1).astype(jnp.int32)


def draw_chaos_index(key, part):
    score_key = jax.random.fold_in(key, 21)
    raw = jax.random.randint(score_key, (NKL, P_SIZE, P_SIZE), 0, 1 << 20, dtype=jnp.int32)
    columns = jnp.arange(P_SIZE, dtype=jnp.int32)
    scores = raw * P_SIZE + columns[None, None, :]
    diagonal = columns[:, None] == columns[None, :]
    scores = jnp.where(diagonal[None, :, :], jnp.int32(-1), scores)
    top_vals, top_index = lax.top_k(scores, NZC - 1)
    own_terms = jnp.broadcast_to(columns[None, :, None], (NKL, P_SIZE, 1))
    return jnp.concatenate([own_terms, top_index.astype(jnp.int32)], axis=2).astype(jnp.int32)


def shard_levels(stream_key, dims, cuts, least, top_value):
    def one(position, shards_of):
        draws = jax.random.uniform(jax.random.fold_in(jax.random.fold_in(stream_key, 6), position), (shards_of,), jnp.float32, least / len(cuts), top_value / len(cuts))
        return jnp.repeat(jnp.exp(draws), dims[position] // shards_of).reshape((-1,) + (1,) * (len(dims) - position - 1))

    level = one(*cuts[0])
    for cut in cuts[1:]:
        level = level * one(*cut)
    return level


def normal_values(own_key, extent, width, bound, shards=(), kind=jnp.bfloat16):
    entries = width * jax.random.normal(own_key, extent, jnp.float32)
    if shards:
        entries = entries * shard_levels(own_key, extent, shards, -0.22, 0.18)
    return jnp.clip(entries, -bound, bound).astype(kind)


def setup_inputs(seed: int = 0) -> dict:
    seeds = jax.random.split(jax.random.key(seed), 6)
    return {
        "load_vectors": normal_values(seeds[0], (P_SIZE, 2, LOADS, NDOF), 1.0, 6.0, ((0, 4), (3, 8))),
        "stiff_tiles": normal_values(seeds[1], (NBLK, NNZ, NKL, 2, TILE, TILE), (TILE * NNZ * NKL * 2) ** -0.5, 0.09375, ((0, 8),)),
        "tile_columns": draw_tile_columns(jax.random.fold_in(seeds[5], 71), 0),
        "chaos_index": draw_chaos_index(jax.random.fold_in(seeds[5], 71), 0),
        "chaos_value": normal_values(seeds[4], (NKL, P_SIZE, NZC), NZC ** -0.5, 1.0),
    }


def dense_term(index_pair):
    row_index, row_value = index_pair
    columns = jnp.arange(P_SIZE, dtype=jnp.int32)
    matches = row_index[:, :, None] == columns[None, None, :]
    summed = jnp.where(matches, row_value[:, :, None].astype(jnp.float32), jnp.float32(0.0)).sum(axis=1)
    return summed.astype(jnp.bfloat16)


def reference(load_vectors, stiff_tiles, tile_columns, chaos_index, chaos_value):
    coupling = lax.map(dense_term, (chaos_index, chaos_value))
    padded = jnp.pad(load_vectors, ((0, 0), (0, 0), (0, 0), (TILE, TILE)))
    flattened = padded.reshape(P_SIZE, -1)
    rows_all = stiff_tiles.shape[0]
    base = (jnp.arange(rows_all, dtype=jnp.int32) // BLK_DEV) * BLK_DEV
    global_cols = (base[:, None] + tile_columns).astype(jnp.int32)
    start_sum = jnp.zeros((P_SIZE, 2, LOADS, rows_all, TILE), jnp.float32)

    def add_term(kl_term, response):
        mixed = jnp.dot(coupling[kl_term], flattened, preferred_element_type=jnp.float32).astype(jnp.bfloat16)
        mixed = mixed.reshape(P_SIZE, 2, LOADS, rows_all + 2, TILE)
        for tile_slot in range(NNZ):
            columns = jnp.take(mixed, global_cols[:, tile_slot], axis=3).astype(jnp.float32)
            tile_k = stiff_tiles[:, tile_slot, kl_term].astype(jnp.float32)
            real_tile = tile_k[:, 0]
            imag_tile = tile_k[:, 1]
            real_out = jnp.einsum("bxy,prby->prbx", real_tile, columns[:, 0]) - jnp.einsum("bxy,prby->prbx", imag_tile, columns[:, 1])
            imag_out = jnp.einsum("bxy,prby->prbx", real_tile, columns[:, 1]) + jnp.einsum("bxy,prby->prbx", imag_tile, columns[:, 0])
            response = response + jnp.stack([real_out, imag_out], axis=1)
        return response

    response = lax.fori_loop(0, NKL, add_term, start_sum)
    return response.reshape(load_vectors.shape)
```

```python
import functools

import jax
import jax.numpy as jnp
from jax import lax
from jax.experimental import pallas as pl
from jax.experimental.pallas import tpu as pltpu
from jax.sharding import PartitionSpec as P

TILE = 96


def coupling_kernel(place_ref, index_ref, value_ref, out_ref):
    me = place_ref[0]
    terms = out_ref.shape[1]
    share = terms // 4
    half = terms // 2

    def arrange(v):
        low, high = v[:, :half], v[:, half:]
        flip = (me >> 1) == 1
        first, second = jnp.where(flip, high, low), jnp.where(flip, low, high)
        shift = (me & 1) * share
        return jnp.concatenate([pltpu.roll(first, shift, 1), pltpu.roll(second, shift, 1)], axis=1)

    index = arrange(index_ref[0] ^ (me * share)).astype(jnp.float32).astype(jnp.bfloat16)
    value = arrange(value_ref[0].astype(jnp.float32)).astype(jnp.bfloat16)
    chunk = terms // 4
    for part in range(terms // chunk):
        j = lax.broadcasted_iota(jnp.int32, (chunk, terms), 0) + part * chunk
        j = j.astype(jnp.float32).astype(jnp.bfloat16)
        dense = jnp.zeros((chunk, terms), jnp.bfloat16)
        for n in range(index.shape[0]):
            dense = jnp.where(index[n : n + 1, :] == j, value[n : n + 1, :], dense)
        out_ref[0, part * chunk : (part + 1) * chunk, :] = dense


def dense_coupling(place, chaos_index, chaos_value):
    nkl, terms, nzc = chaos_index.shape
    return pl.pallas_call(
        coupling_kernel,
        grid_spec=pltpu.PrefetchScalarGridSpec(
            num_scalar_prefetch=1,
            grid=(nkl,),
            in_specs=[pl.BlockSpec((1, nzc, terms), lambda k, w: (k, 0, 0))] * 2,
            out_specs=pl.BlockSpec((1, terms, terms), lambda k, w: (k, 0, 0)),
        ),
        out_shape=jax.ShapeDtypeStruct((nkl, terms, terms), jnp.bfloat16),
        cost_estimate=pl.CostEstimate(flops=10_000_000, bytes_accessed=2_000_000, transcendentals=0),
    )(place, jnp.swapaxes(chaos_index, 1, 2), jnp.swapaxes(chaos_value, 1, 2))


def tiles_kernel(tiles_ref, out_ref):
    _, nnz, nkl = tiles_ref.shape[:3]
    for s in range(nnz):
        for part in range(2):
            out_ref[0, s, part * TILE : (part + 1) * TILE, :] = jnp.concatenate(
                [tiles_ref[0, s, k, part] for k in range(nkl)], axis=1
            )


def wide_tiles(stiff_tiles):
    blocks, nnz, nkl = stiff_tiles.shape[:3]
    return pl.pallas_call(
        tiles_kernel,
        grid=(blocks,),
        in_specs=[pl.BlockSpec((1, nnz, nkl, 2, TILE, TILE), lambda b: (b, 0, 0, 0, 0, 0))],
        out_specs=pl.BlockSpec((1, nnz, 2 * TILE, nkl * TILE), lambda b: (b, 0, 0, 0)),
        out_shape=jax.ShapeDtypeStruct((blocks, nnz, 2 * TILE, nkl * TILE), jnp.bfloat16),
        cost_estimate=pl.CostEstimate(flops=10_000_000, bytes_accessed=4_000_000, transcendentals=0),
    )(stiff_tiles)


def pack_kernel(chunk, place_ref, own_ref, near_ref, keep_ref, send_ref, rows):
    me = place_ref[0]
    terms, _, loads, width = own_ref.shape
    lanes = rows.shape[3]
    for which, ref in enumerate((own_ref, near_ref)):
        for t in range(width // lanes):
            part = ref[:, 0, :, t * lanes : (t + 1) * lanes].astype(jnp.float32)
            rows[which, t] = part.reshape(terms * loads, lanes)
    for m in range(keep_ref.shape[0]):
        for out_ref, x in ((send_ref, 1 - (me >> 1)), (keep_ref, me >> 1)):
            r = 8 * chunk + 4 * m + 2 * (me & 1) + x
            for t in range(width // lanes):
                both = [rows[which, t, pl.ds(r, terms, stride=loads), :] for which in range(2)]
                flipped = jnp.concatenate(both, axis=0).astype(jnp.bfloat16).T
                out_ref[m, 0, t * lanes : (t + 1) * lanes, :] = flipped


def pack(place, own, near, chunk):
    terms, parts, loads, width = own.shape
    cases = loads // 8
    out = jax.ShapeDtypeStruct((cases, parts, width, 2 * terms), jnp.bfloat16)
    return pl.pallas_call(
        functools.partial(pack_kernel, chunk),
        grid_spec=pltpu.PrefetchScalarGridSpec(
            num_scalar_prefetch=1,
            grid=(parts,),
            in_specs=[pl.BlockSpec((terms, 1, loads, width), lambda c, w: (0, c, 0, 0))] * 2,
            out_specs=[pl.BlockSpec((cases, 1, width, 2 * terms), lambda c, w: (0, c, 0, 0))] * 2,
            scratch_shapes=[pltpu.VMEM((2, width // 128, terms * loads, 128), jnp.float32)],
        ),
        out_shape=[out, out],
        compiler_params=pltpu.CompilerParams(vmem_limit_bytes=24 << 20),
        cost_estimate=pl.CostEstimate(flops=1_000_000, bytes_accessed=4_000_000, transcendentals=0),
    )(place, own, near)


def operator_kernel(slots_ref, own_ref, far_ref, even_ref, odd_ref, coupling_ref, tiles_ref, keep_ref, send_ref, mixed):
    nkl, terms, _ = coupling_ref.shape
    blocks, nnz = tiles_ref.shape[:2]
    half = terms // 2
    for c in range(2):
        pieces = [jnp.concatenate([own_ref[0, c], far_ref[0, c]], axis=1)]
        for halo_ref in (even_ref, odd_ref):
            pieces.append(jnp.concatenate([halo_ref[0, 0, c], halo_ref[0, 1, c]], axis=1))
        field = jnp.concatenate(pieces, axis=0)
        for k in range(nkl):
            mix = jnp.dot(field, coupling_ref[k], preferred_element_type=jnp.float32).astype(jnp.bfloat16)
            for g in range(blocks + 2):
                mixed[g, k * TILE : (k + 1) * TILE, c * terms : (c + 1) * terms] = mix[g * TILE : (g + 1) * TILE]
    for b in range(blocks):
        acc = None
        for s in range(nnz):
            term = jnp.dot(tiles_ref[b, s], mixed[slots_ref[b * nnz + s]], preferred_element_type=jnp.float32)
            acc = term if acc is None else acc + term
        real = (acc[:TILE, :terms] - acc[TILE:, terms:]).T.astype(jnp.bfloat16)
        imag = (acc[:TILE, terms:] + acc[TILE:, :terms]).T.astype(jnp.bfloat16)
        for c, part in enumerate((real, imag)):
            keep_ref[0, c, :, b * TILE : (b + 1) * TILE] = part[:half]
            send_ref[0, c, :, b * TILE : (b + 1) * TILE] = part[half:]


def apply_operator(slots, own, far, even, odd, coupling, tiles):
    cases, _, width, half = own.shape
    blocks, _, _, depth = tiles.shape
    terms = coupling.shape[1]
    inner = pl.BlockSpec((1, 2, width, half), lambda r, s: (r, 0, 0, 0))
    outer = pl.BlockSpec((1, 2, 2, TILE, half), lambda r, s: (r, 0, 0, 0, 0))
    out = jax.ShapeDtypeStruct((cases, 2, half, width), jnp.bfloat16)
    return pl.pallas_call(
        operator_kernel,
        grid_spec=pltpu.PrefetchScalarGridSpec(
            num_scalar_prefetch=1,
            grid=(cases,),
            in_specs=[
                inner,
                inner,
                outer,
                outer,
                pl.BlockSpec(coupling.shape, lambda r, s: (0, 0, 0)),
                pl.BlockSpec(tiles.shape, lambda r, s: (0, 0, 0, 0)),
            ],
            out_specs=[pl.BlockSpec((1, 2, half, width), lambda r, s: (r, 0, 0, 0))] * 2,
            scratch_shapes=[pltpu.VMEM((blocks + 2, depth, 2 * terms), jnp.bfloat16)],
        ),
        out_shape=[out, out],
        compiler_params=pltpu.CompilerParams(vmem_limit_bytes=32 << 20),
        cost_estimate=pl.CostEstimate(flops=6_000_000_000, bytes_accessed=5_000_000, transcendentals=0),
    )(slots, own, far, even, odd, coupling, tiles)


def unpack_kernel(place_ref, *refs):
    me = place_ref[0]
    *piece_refs, out_ref, rows = refs
    cases, parts, terms, width = piece_refs[0].shape
    lanes = rows.shape[2]
    loads = out_ref.shape[0] // (terms * parts)
    for position, ref in enumerate(piece_refs):
        chunk, source = position // 4, me ^ (position % 4)
        for m in range(cases):
            r = 8 * chunk + 4 * m + 2 * (source & 1) + (source >> 1)
            for c in range(parts):
                for t in range(width // lanes):
                    part = ref[m, c, :, t * lanes : (t + 1) * lanes].astype(jnp.float32)
                    rows[t, pl.ds(c * loads + r, terms, stride=parts * loads), :] = part
    for t in range(width // lanes):
        out_ref[:, t * lanes : (t + 1) * lanes] = rows[t]


def unpack(place, chunks):
    cases, parts, half, width = chunks[0][0].shape
    terms = half // 2
    loads = 4 * cases * len(chunks)
    step = 16
    steps = terms // step
    first = pl.BlockSpec((cases, parts, step, width), lambda t, w: (0, 0, t, 0))
    second = pl.BlockSpec((cases, parts, step, width), lambda t, w: (0, 0, t + steps, 0))
    pieces, specs = [], []
    for keep, near_keep, back, near_back in chunks:
        pieces += [keep, near_keep, back, near_back]
        specs += [first, second, first, second]
    out = pl.pallas_call(
        unpack_kernel,
        grid_spec=pltpu.PrefetchScalarGridSpec(
            num_scalar_prefetch=1,
            grid=(steps,),
            in_specs=specs,
            out_specs=pl.BlockSpec((step * parts * loads, width), lambda t, w: (t, 0)),
            scratch_shapes=[pltpu.VMEM((width // 128, step * parts * loads, 128), jnp.float32)],
        ),
        out_shape=jax.ShapeDtypeStruct((terms * parts * loads, width), jnp.float32),
        cost_estimate=pl.CostEstimate(flops=1_000_000, bytes_accessed=6_000_000, transcendentals=0),
    )(place, *pieces)
    return out.reshape(terms, parts, loads, width)


def swap_edges(own, far):
    count = lax.axis_size("space")
    odd_place = lax.axis_index("space") % 2
    last = own.shape[2] - TILE

    def edge(start):
        return jnp.stack([lax.dynamic_slice_in_dim(v, start, TILE, axis=2) for v in (own, far)], axis=1)

    even_pairs = [(i, i ^ 1) for i in range(count)]
    odd_pairs = [(i, ((i - 1) ^ 1) + 1) for i in range(1, count - 1)]
    even = lax.ppermute(edge(last * (1 - odd_place)), "space", even_pairs)
    odd = lax.ppermute(edge(last * odd_place), "space", odd_pairs)
    return even, odd


def body(load_vectors, stiff_tiles, tile_columns, chaos_index, chaos_value):
    count = lax.axis_size("chaos")
    blocks = stiff_tiles.shape[0]
    odd_place = lax.axis_index("space") % 2
    slots = jnp.where(
        tile_columns == 0,
        blocks + 1 - odd_place,
        jnp.where(tile_columns == blocks + 1, blocks + odd_place, tile_columns - 1),
    ).reshape(-1)

    if count != 4:
        coupling = dense_coupling(jnp.zeros((1,), jnp.int32), chaos_index, chaos_value)
        tiles = wide_tiles(stiff_tiles)
        mine = lax.all_to_all(load_vectors, "chaos", split_axis=2, concat_axis=0, tiled=True)
        mine = mine.transpose(2, 1, 3, 0)
        half = mine.shape[3] // 2
        own, far = mine[..., :half], mine[..., half:]
        even, odd = swap_edges(own, far)
        keep, send = apply_operator(slots, own, far, even, odd, coupling, tiles)
        result = jnp.concatenate([keep, send], axis=2)
        result = lax.all_to_all(result, "chaos", split_axis=2, concat_axis=0, tiled=True)
        return result.transpose(2, 1, 0, 3).astype(jnp.float32)

    place = lax.axis_index("chaos").reshape(1)
    near = lambda v: lax.ppermute(v, "chaos", [(i, i ^ 1) for i in range(4)])
    across = lambda v: lax.ppermute(v, "chaos", [(i, i ^ 2) for i in range(4)])
    near_loads = near(load_vectors)
    tiles = wide_tiles(stiff_tiles)
    packed = [pack(place, load_vectors, near_loads, chunk) for chunk in range(2)]
    far = [across(send) for _, send in packed]
    coupling = dense_coupling(place, chaos_index, chaos_value)
    chunks = []
    for (own, _), other in zip(packed, far):
        even, odd = swap_edges(own, other)
        keep, send = apply_operator(slots, own, other, even, odd, coupling, tiles)
        back = across(send)
        chunks.append((keep, near(keep), back, near(back)))
    return unpack(place, chunks)


def solution(mesh):
    in_specs = (
        P("chaos", None, None, "space"),
        P("space", None, None, None, None, None),
        P("space", None),
        P(),
        P(),
    )
    out_specs = P("chaos", None, None, "space")
    return jax.shard_map(body, mesh=mesh, in_specs=in_specs, out_specs=out_specs, check_vma=False)
```

```python
import functools

import jax
import jax.numpy as jnp
from jax import lax
from jax.experimental import pallas as pl
from jax.experimental.pallas import tpu as pltpu
from jax.sharding import PartitionSpec as P

TILE = 96
VMEM = pl.BlockSpec(memory_space=pltpu.VMEM)
SMEM = pl.BlockSpec(memory_space=pltpu.SMEM)
ANY = pl.BlockSpec(memory_space=pl.ANY)
HBM = pl.BlockSpec(memory_space=pltpu.HBM)
SHORT = pl.CostEstimate(flops=1000, bytes_accessed=1000, transcendentals=0)


def near_core(*values):
    return [pltpu.with_memory_space_constraint(v, pltpu.VMEM) for v in values]


def in_hbm(value):
    return pltpu.with_memory_space_constraint(value, pltpu.HBM)


def params(mebibytes):
    return pltpu.CompilerParams(vmem_limit_bytes=mebibytes << 20)


def coupling_kernel(place_ref, index_hbm_ref, value_hbm_ref, out_ref, index_ref, value_ref, done):
    copies = [
        pltpu.make_async_copy(index_hbm_ref, index_ref, done.at[0]),
        pltpu.make_async_copy(value_hbm_ref, value_ref, done.at[1]),
    ]
    for copy in copies:
        copy.start()
    for copy in copies:
        copy.wait()
    me = place_ref[0]
    nkl, terms, _ = out_ref.shape
    share = terms // 4
    half = terms // 2

    def arrange(v):
        low, high = v[:, :half], v[:, half:]
        flip = (me >> 1) == 1
        first, second = jnp.where(flip, high, low), jnp.where(flip, low, high)
        shift = (me & 1) * share
        return jnp.concatenate([pltpu.roll(first, shift, 1), pltpu.roll(second, shift, 1)], axis=1)

    def one_term(k, carry):
        index = arrange(index_ref[k] ^ (me * share)).astype(jnp.float32).astype(jnp.bfloat16)
        value = arrange(value_ref[k].astype(jnp.float32)).astype(jnp.bfloat16)
        chunk = terms // 4
        for part in range(terms // chunk):
            j = lax.broadcasted_iota(jnp.int32, (chunk, terms), 0) + part * chunk
            j = j.astype(jnp.float32).astype(jnp.bfloat16)
            dense = jnp.zeros((chunk, terms), jnp.bfloat16)
            for n in range(index.shape[0]):
                dense = jnp.where(index[n : n + 1, :] == j, value[n : n + 1, :], dense)
            out_ref[k, part * chunk : (part + 1) * chunk, :] = dense
        return carry

    lax.fori_loop(0, nkl, one_term, 0)


def dense_coupling(place, chaos_index, chaos_value):
    nkl, terms, nzc = chaos_index.shape
    return pl.pallas_call(
        coupling_kernel,
        in_specs=[SMEM, ANY, ANY],
        out_specs=VMEM,
        scratch_shapes=[
            pltpu.VMEM((nkl, nzc, terms), chaos_index.dtype),
            pltpu.VMEM((nkl, nzc, terms), chaos_value.dtype),
            pltpu.SemaphoreType.DMA((2,)),
        ],
        out_shape=pltpu.VMEM((nkl, terms, terms), jnp.bfloat16),
        compiler_params=params(8),
        cost_estimate=SHORT,
    )(place, in_hbm(jnp.swapaxes(chaos_index, 1, 2)), in_hbm(jnp.swapaxes(chaos_value, 1, 2)))


def tiles_kernel(_, tiles_hbm_ref, out_ref, tiles_ref, done):
    blocks, nnz, nkl = tiles_ref.shape[:3]
    copies = [pltpu.make_async_copy(tiles_hbm_ref.at[b], tiles_ref.at[b], done.at[b]) for b in range(blocks)]
    for copy in copies:
        copy.start()
    for b in range(blocks):
        copies[b].wait()
        for s in range(nnz):
            for part in range(2):
                out_ref[b, s, part * TILE : (part + 1) * TILE, :] = jnp.concatenate(
                    [tiles_ref[b, s, k, part] for k in range(nkl)], axis=1
                )


def wide_tiles(place, stiff_tiles):
    blocks, nnz, nkl = stiff_tiles.shape[:3]
    return pl.pallas_call(
        tiles_kernel,
        in_specs=[SMEM, ANY],
        out_specs=VMEM,
        scratch_shapes=[pltpu.VMEM(stiff_tiles.shape, stiff_tiles.dtype), pltpu.SemaphoreType.DMA((blocks,))],
        out_shape=pltpu.VMEM((blocks, nnz, 2 * TILE, nkl * TILE), jnp.bfloat16),
        compiler_params=params(8),
        cost_estimate=SHORT,
    )(place, in_hbm(stiff_tiles))


def pack_kernel(place_ref, own_ref, near_ref, *refs):
    out_refs, (staged, rows, done), packed = refs[:6], refs[6:9], refs[9:]
    (send_outer, send_inner, keep_outer, keep_inner), pair_refs = packed[:4], packed[4:]
    me, odd_place = place_ref[0], place_ref[1] == 1
    terms, parts, loads, width = own_ref.shape
    copies = [
        [pltpu.make_async_copy(ref.at[:, c], staged.at[q, :, c], done.at[2 * c + q]) for q, ref in enumerate((own_ref, near_ref))]
        for c in range(parts)
    ]
    for pair in copies:
        for copy in pair:
            copy.start()
    out_copies = []
    cases = loads // 4
    lanes = rows.shape[3]
    for c in range(parts):
        for copy in copies[c]:
            copy.wait()
        for t in range(width // lanes):
            for q in range(2):
                piece = staged[q, :, c, :, t * lanes : (t + 1) * lanes].astype(jnp.float32)
                rows[c, t, q * terms * loads : (q + 1) * terms * loads] = piece.reshape(terms * loads, lanes)
            first, last = t * lanes, (t + 1) * lanes
            for m in range(cases):
                for outer, inner, x in ((send_outer, send_inner, 1 - (me >> 1)), (keep_outer, keep_inner, me >> 1)):
                    r = 4 * m + 2 * (me & 1) + x
                    both = rows[c, t, pl.ds(r, 2 * terms, stride=loads), :].astype(jnp.bfloat16).T
                    for ref, low, high, base in (
                        (outer, 0, TILE, 0),
                        (inner, TILE, width - TILE, 0),
                        (outer, width - TILE, width, TILE),
                    ):
                        low_row, high_row = max(low, first), min(high, last)
                        if low_row < high_row:
                            ref[m, c, base + low_row - low : base + high_row - low] = both[low_row - first : high_row - first]
        for m in range(cases):
            low, high = keep_outer[m, c, :TILE], keep_outer[m, c, TILE:]
            pair_refs[0][m, c] = jnp.where(odd_place, low, high)
            pair_refs[1][m, c] = jnp.where(odd_place, high, low)
        for i, (source, target) in enumerate(zip(packed, out_refs)):
            out_copies.append(pltpu.make_async_copy(source.at[:, c], target.at[:, c], done.at[2 * parts + 6 * c + i]))
            out_copies[-1].start()
    for copy in out_copies:
        copy.wait()


def pack(place, own, near):
    terms, parts, loads, width = own.shape
    cases = loads // 4
    shapes = [(cases, parts, 2 * TILE, 2 * terms), (cases, parts, width - 2 * TILE, 2 * terms)] * 2
    shapes += [(cases, parts, TILE, 2 * terms)] * 2
    return pl.pallas_call(
        pack_kernel,
        in_specs=[SMEM, ANY, ANY],
        out_specs=[HBM] * 6,
        scratch_shapes=[
            pltpu.VMEM((2, *near.shape), near.dtype),
            pltpu.VMEM((parts, width // 128, 2 * terms * loads, 128), jnp.float32),
            pltpu.SemaphoreType.DMA((8 * parts,)),
            *[pltpu.VMEM(shape, near.dtype) for shape in shapes],
        ],
        out_shape=[pltpu.HBM(shape, near.dtype) for shape in shapes],
        compiler_params=params(20),
        cost_estimate=SHORT,
    )(place, in_hbm(own), near)


def outer_kernel(place_ref, own_ref, far_ref, field_ref, even_ref, odd_ref, done):
    odd_place = place_ref[1] == 1
    cases, parts, _, half = own_ref.shape
    copies = [
        pltpu.make_async_copy(ref, field_ref.at[:, :, :, pl.ds(q * half, half)], done.at[q])
        for q, ref in ((1, far_ref), (0, own_ref))
    ]
    for copy in copies:
        copy.start()
    copies[0].wait()
    for m in range(cases):
        for c in range(parts):
            low, high = field_ref[m, c, :TILE, half:], field_ref[m, c, TILE:, half:]
            even_ref[m, c] = jnp.where(odd_place, low, high)
            odd_ref[m, c] = jnp.where(odd_place, high, low)
    copies[1].wait()


def gather_outer(place, own, far):
    cases, parts, height, half = own.shape
    edge = pltpu.VMEM((cases, parts, TILE, half), jnp.bfloat16)
    return pl.pallas_call(
        outer_kernel,
        in_specs=[SMEM, ANY, ANY],
        out_specs=[VMEM] * 3,
        scratch_shapes=[pltpu.SemaphoreType.DMA((2,))],
        out_shape=[pltpu.VMEM((cases, parts, height, 2 * half), jnp.bfloat16), edge, edge],
        compiler_params=params(4),
        cost_estimate=SHORT,
    )(place, in_hbm(own), far)


def swap(even, odd):
    count = lax.axis_size("space")
    even_pairs = [(i, i ^ 1) for i in range(count)]
    odd_pairs = [(i, ((i - 1) ^ 1) + 1) for i in range(1, count - 1)]
    return lax.ppermute(even, "space", even_pairs), lax.ppermute(odd, "space", odd_pairs)


def mix(fields, coupling_ref, slots, mixed):
    nkl, terms, _ = coupling_ref.shape
    for k in range(nkl):
        rows = slice(k * TILE, (k + 1) * TILE)
        for c, field in enumerate(fields):
            sums = jnp.dot(field, coupling_ref[k], preferred_element_type=jnp.float32).astype(jnp.bfloat16)
            for g, slot in enumerate(slots):
                mixed[slot, rows, c * terms : (c + 1) * terms] = sums[g * TILE : (g + 1) * TILE]


def mix_outer_kernel(field_ref, coupling_ref, mixed):
    def one_case(m, carry):
        mix([field_ref[m, c] for c in range(2)], coupling_ref, (0, mixed.shape[1] - 3), mixed.at[m])
        return carry

    lax.fori_loop(0, field_ref.shape[0], one_case, 0)


def mix_outer(field, coupling, blocks):
    cases, _, height, terms = field.shape
    nkl = coupling.shape[0]
    return pl.pallas_call(
        mix_outer_kernel,
        in_specs=[VMEM] * 2,
        out_specs=VMEM,
        out_shape=pltpu.VMEM((cases, blocks + 2, nkl * TILE, 2 * terms), jnp.bfloat16),
        compiler_params=params(4),
        cost_estimate=SHORT,
    )(*near_core(field, coupling))


def mix_inner_kernel(own_ref, far_ref, *refs):
    edge_refs = refs[: (len(refs) - 5) // 2]
    coupling_ref, _, mixed, *staged_refs, field_ref, done = refs[len(edge_refs) :]
    half = own_ref.shape[3]
    pairs = [
        (far_ref, field_ref.at[:, :, :, pl.ds(half, half)]),
        (own_ref, field_ref.at[:, :, :, pl.ds(0, half)]),
        *zip(edge_refs, staged_refs),
    ]
    copies = [pltpu.make_async_copy(source, target, done.at[i]) for i, (source, target) in enumerate(pairs)]
    for copy in copies:
        copy.start()
    for copy in copies[:2]:
        copy.wait()

    def one_case(m, carry):
        mix([field_ref[m, c] for c in range(2)], coupling_ref, range(1, mixed.shape[1] - 3), mixed.at[m])
        return carry

    lax.fori_loop(0, field_ref.shape[0], one_case, 0)
    for copy in copies[2:]:
        copy.wait()


def mix_inner(own, far, edges, coupling, mixed):
    cases, parts, height, half = own.shape
    nkl, terms, _ = coupling.shape
    count = len(edges)
    return pl.pallas_call(
        mix_inner_kernel,
        in_specs=[ANY] * (2 + count) + [VMEM] * 2,
        out_specs=[VMEM] * (1 + count),
        scratch_shapes=[
            pltpu.VMEM((cases, parts, height, terms), jnp.bfloat16),
            pltpu.SemaphoreType.DMA((2 + count,)),
        ],
        out_shape=[pltpu.VMEM(mixed.shape, mixed.dtype)] + [pltpu.VMEM(v.shape, v.dtype) for v in edges],
        input_output_aliases={3 + count: 0},
        compiler_params=params(8),
        cost_estimate=SHORT,
    )(in_hbm(own), far, *edges, *near_core(coupling, mixed))


def tiles_apply_kernel(m, quarters, place_ref, columns_ref, *refs):
    *edge_refs, coupling_ref, tiles_ref, _ = refs[:7]
    *out_refs, whole, flipped = refs[7:]
    terms = coupling_ref.shape[1]
    blocks, nnz = tiles_ref.shape[:2]
    half = terms // 2
    low, high = half * quarters[0], half * (quarters[-1] + 1)
    mixed = whole.at[m]

    def outer(c):
        even, odd, far_even, far_odd = (ref[m, c] for ref in edge_refs)
        return jnp.concatenate(
            [jnp.concatenate([even, far_even], axis=1), jnp.concatenate([odd, far_odd], axis=1)], axis=0
        )

    def slot_of(column):
        odd_place = place_ref[1]
        outside = jnp.where(column == 0, blocks + 1 - odd_place, blocks + odd_place)
        return jnp.where((column == 0) | (column == blocks + 1), outside, column - 1)

    if quarters[-1] == 1:
        mix([outer(c) for c in range(2)], coupling_ref, (blocks, blocks + 1), mixed)
    count = high - low
    for b in range(blocks):
        acc = None
        for s in range(nnz):
            slot = slot_of(columns_ref[b, s])
            field = jnp.concatenate([mixed[slot, :, c * terms + low : c * terms + high] for c in range(2)], axis=1)
            term = jnp.dot(tiles_ref[b, s], field, preferred_element_type=jnp.float32)
            acc = term if acc is None else acc + term
        rows = slice(b * TILE, (b + 1) * TILE)
        flipped[0, rows, :count] = (acc[:TILE, :count] - acc[TILE:, count:]).astype(jnp.bfloat16)
        flipped[1, rows, :count] = (acc[:TILE, count:] + acc[TILE:, :count]).astype(jnp.bfloat16)
    for c in range(2):
        part = flipped[c, :, :count].T
        for i, ref in enumerate(out_refs):
            ref[c] = part[i * half : (i + 1) * half]


def apply_tiles(m, place, columns, edges, coupling, tiles, mixed, quarters=(0, 1)):
    blocks, nnz, rows, depth = tiles.shape
    terms = coupling.shape[1]
    out = pltpu.VMEM((2, terms // 2, blocks * TILE), jnp.bfloat16)
    count = len(quarters)
    return pl.pallas_call(
        functools.partial(tiles_apply_kernel, m, quarters),
        in_specs=[SMEM] * 2 + [VMEM] * 7,
        out_specs=[VMEM] * (count + 1),
        scratch_shapes=[pltpu.VMEM((2, blocks * TILE, terms), jnp.bfloat16)],
        out_shape=[out] * count + [pltpu.VMEM(mixed.shape, mixed.dtype)],
        input_output_aliases={8: count},
        compiler_params=params(8),
        cost_estimate=SHORT,
    )(place, columns, *near_core(*edges, coupling, tiles, mixed))


def unpack_kernel(chunk, place_ref, *refs):
    me = place_ref[0]
    *piece_refs, out_ref, rows, done = refs
    parts, half, width = piece_refs[0].shape
    terms = half // 2
    loads = out_ref.shape[1] // 2
    lanes = rows.shape[2]
    copies = []
    for t in range(width // lanes):
        for position in range(loads):
            m, source = position // 4, me ^ (position % 4)
            r = 4 * m + 2 * (source & 1) + (source >> 1)
            first = terms * (position % 2)
            for c in range(parts):
                part = piece_refs[position][c, first : first + terms, t * lanes : (t + 1) * lanes]
                rows[t, pl.ds(c * loads + r, terms, stride=parts * loads), :] = part.astype(jnp.float32)
        source = rows.at[t].reshape(terms * parts, loads, lanes)
        target = out_ref.at[:, loads * chunk : loads * (chunk + 1), t * lanes : (t + 1) * lanes]
        copies.append(pltpu.make_async_copy(source, target, done.at[t]))
        copies[-1].start()
    for copy in copies:
        copy.wait()


def unpack(place, chunk, pieces, whole=None):
    parts, half, width = pieces[0].shape
    terms = half // 2
    loads = len(pieces)
    specs = [SMEM] + [VMEM] * loads
    aliases = {}
    if whole is not None:
        aliases = {len(pieces) + 1: 0}
        pieces = [*pieces, whole]
        specs = [*specs, ANY]

    def kernel(place_ref, *refs):
        refs = list(refs)
        if aliases:
            refs.pop(loads)
        unpack_kernel(chunk, place_ref, *refs)

    return pl.pallas_call(
        kernel,
        in_specs=specs,
        out_specs=ANY,
        scratch_shapes=[
            pltpu.VMEM((width // 128, terms * parts * loads, 128), jnp.float32),
            pltpu.SemaphoreType.DMA((width // 128,)),
        ],
        out_shape=jax.ShapeDtypeStruct((terms * parts, 2 * loads, width), jnp.float32),
        input_output_aliases=aliases,
        compiler_params=params(8),
        cost_estimate=SHORT,
    )(place, *pieces)


def after(value, *others):
    return lax.optimization_barrier((value, others))[0]


def body(load_vectors, stiff_tiles, tile_columns, chaos_index, chaos_value):
    count = lax.axis_size("chaos")
    blocks = stiff_tiles.shape[0]
    odd_place = lax.axis_index("space") % 2

    if count != 4:
        place = jnp.stack([jnp.zeros((), jnp.int32), odd_place])
        coupling = dense_coupling(place, chaos_index, chaos_value)
        tiles = wide_tiles(place, stiff_tiles)
        mine = lax.all_to_all(load_vectors, "chaos", split_axis=2, concat_axis=0, tiled=True)
        field = mine.transpose(2, 1, 3, 0)
        half = field.shape[3] // 2
        low, high = field[:, :, :TILE], field[:, :, -TILE:]
        swapped = swap(jnp.where(odd_place == 1, low, high), jnp.where(odd_place == 1, high, low))
        edges = [v[..., :half] for v in swapped] + [v[..., half:] for v in swapped]
        inner = field[:, :, TILE:-TILE]
        mixed = mix_outer(jnp.concatenate([low, high], axis=2), coupling, blocks)
        mixed = mix_inner(inner[..., :half], inner[..., half:], [], coupling, mixed)[0]
        cases = []
        for m in range(field.shape[0]):
            keep, send, mixed = apply_tiles(m, place, tile_columns, edges, coupling, tiles, mixed)
            cases.append(jnp.concatenate([keep, send], axis=1))
        result = jnp.stack(cases, axis=0)
        result = lax.all_to_all(result, "chaos", split_axis=2, concat_axis=0, tiled=True)
        return result.transpose(2, 1, 0, 3).astype(jnp.float32)

    place = jnp.stack([lax.axis_index("chaos"), odd_place])
    near = lambda v: lax.ppermute(v, "chaos", [(i, i ^ 1) for i in range(4)])
    across = lambda v: lax.ppermute(v, "chaos", [(i, i ^ 2) for i in range(4)])
    near_loads = near(load_vectors)
    coupling = dense_coupling(place, chaos_index, chaos_value)
    place = after(place, coupling)
    send_outer, send_inner, outer, inner, even, odd = pack(place, load_vectors, near_loads)
    far_outer = across(send_outer)
    own_edges = swap(even, odd)
    tiles = wide_tiles(after(place, even), stiff_tiles)
    far_inner = across(after(send_inner, tiles))
    field, even, odd = gather_outer(after(place, tiles), outer, far_outer)
    far_edges = swap(even, odd)
    mixed = mix_outer(field, coupling, blocks)
    mixed, *own_edges = mix_inner(inner, far_inner, own_edges, coupling, mixed)
    cases = field.shape[0]
    edges = [*own_edges, *far_edges]
    kept, near_kept, sent = [], [], []
    for m in range(cases):
        ready = after(place, *near_kept[m - 2 : m - 1], *sent[m - 3 : m - 2]) if m >= 2 else place
        given = ready, tile_columns, edges, coupling, tiles
        if m < cases - 1:
            keep, send, mixed = apply_tiles(m, *given, mixed)
        else:
            send, mixed = apply_tiles(m, *given, mixed, (1,))
            keep, mixed = apply_tiles(m, after(place, near_kept[m - 1], sent[m - 2]), *given[1:], mixed, (0,))
        kept.append(keep)
        near_kept.append(near(keep))
        sent.append(across(send))
    result = None
    for chunk in range(2):
        pieces = []
        for m in (2 * chunk, 2 * chunk + 1):
            back = after(sent[m], kept[-1] if result is None else result)
            pieces += [kept[m], near_kept[m], back, near(back)]
        result = unpack(after(place, sent[2]), chunk, pieces, result)
    return result.reshape(load_vectors.shape)


def solution(mesh):
    in_specs = (
        P("chaos", None, None, "space"),
        P("space", None, None, None, None, None),
        P("space", None),
        P(),
        P(),
    )
    out_specs = P("chaos", None, None, "space")
    return jax.shard_map(body, mesh=mesh, in_specs=in_specs, out_specs=out_specs, check_vma=False)
```

```python
import functools

import jax
import jax.numpy as jnp
from jax import lax
from jax.experimental import pallas as pl
from jax.experimental.pallas import tpu as pltpu
from jax.sharding import PartitionSpec as P

TILE = 96
VMEM = pl.BlockSpec(memory_space=pltpu.VMEM)
SMEM = pl.BlockSpec(memory_space=pltpu.SMEM)
ANY = pl.BlockSpec(memory_space=pl.ANY)
HBM = pl.BlockSpec(memory_space=pltpu.HBM)
SHORT = pl.CostEstimate(flops=1000, bytes_accessed=1000, transcendentals=0)


def near_core(*values):
    return [pltpu.with_memory_space_constraint(v, pltpu.VMEM) for v in values]


def in_hbm(value):
    return pltpu.with_memory_space_constraint(value, pltpu.HBM)


def params(mebibytes):
    return pltpu.CompilerParams(vmem_limit_bytes=mebibytes << 20)


def coupling_kernel(place_ref, index_hbm_ref, value_hbm_ref, out_ref, index_ref, value_ref, done):
    copies = [
        pltpu.make_async_copy(index_hbm_ref, index_ref, done.at[0]),
        pltpu.make_async_copy(value_hbm_ref, value_ref, done.at[1]),
    ]
    for copy in copies:
        copy.start()
    for copy in copies:
        copy.wait()
    me = place_ref[0]
    nkl, terms, _ = out_ref.shape
    share = terms // 4
    half = terms // 2

    def arrange(v):
        low, high = v[:, :half], v[:, half:]
        flip = (me >> 1) == 1
        first, second = jnp.where(flip, high, low), jnp.where(flip, low, high)
        shift = (me & 1) * share
        return jnp.concatenate([pltpu.roll(first, shift, 1), pltpu.roll(second, shift, 1)], axis=1)

    def one_term(k, carry):
        index = arrange(index_ref[k] ^ (me * share)).astype(jnp.float32).astype(jnp.bfloat16)
        value = arrange(value_ref[k].astype(jnp.float32)).astype(jnp.bfloat16)
        chunk = terms // 4
        for part in range(terms // chunk):
            j = lax.broadcasted_iota(jnp.int32, (chunk, terms), 0) + part * chunk
            j = j.astype(jnp.float32).astype(jnp.bfloat16)
            dense = jnp.zeros((chunk, terms), jnp.bfloat16)
            for n in range(index.shape[0]):
                dense = jnp.where(index[n : n + 1, :] == j, value[n : n + 1, :], dense)
            out_ref[k, part * chunk : (part + 1) * chunk, :] = dense
        return carry

    lax.fori_loop(0, nkl, one_term, 0)


def dense_coupling(place, chaos_index, chaos_value):
    nkl, terms, nzc = chaos_index.shape
    return pl.pallas_call(
        coupling_kernel,
        in_specs=[SMEM, ANY, ANY],
        out_specs=VMEM,
        scratch_shapes=[
            pltpu.VMEM((nkl, nzc, terms), chaos_index.dtype),
            pltpu.VMEM((nkl, nzc, terms), chaos_value.dtype),
            pltpu.SemaphoreType.DMA((2,)),
        ],
        out_shape=pltpu.VMEM((nkl, terms, terms), jnp.bfloat16),
        compiler_params=params(8),
        cost_estimate=SHORT,
    )(place, in_hbm(jnp.swapaxes(chaos_index, 1, 2)), in_hbm(jnp.swapaxes(chaos_value, 1, 2)))


def tiles_kernel(_, tiles_hbm_ref, out_ref, tiles_ref, done):
    blocks, nnz, nkl = tiles_ref.shape[:3]
    copies = [pltpu.make_async_copy(tiles_hbm_ref.at[b], tiles_ref.at[b], done.at[b]) for b in range(blocks)]
    for copy in copies:
        copy.start()
    for b in range(blocks):
        copies[b].wait()
        for s in range(nnz):
            for part in range(2):
                out_ref[b, s, part * TILE : (part + 1) * TILE, :] = jnp.concatenate(
                    [tiles_ref[b, s, k, part] for k in range(nkl)], axis=1
                )


def wide_tiles(place, stiff_tiles):
    blocks, nnz, nkl = stiff_tiles.shape[:3]
    return pl.pallas_call(
        tiles_kernel,
        in_specs=[SMEM, ANY],
        out_specs=VMEM,
        scratch_shapes=[pltpu.VMEM(stiff_tiles.shape, stiff_tiles.dtype), pltpu.SemaphoreType.DMA((blocks,))],
        out_shape=pltpu.VMEM((blocks, nnz, 2 * TILE, nkl * TILE), jnp.bfloat16),
        compiler_params=params(8),
        cost_estimate=SHORT,
    )(place, in_hbm(stiff_tiles))


def pack_kernel(place_ref, own_ref, near_ref, *refs):
    out_refs, (staged, rows, done), packed = refs[:6], refs[6:9], refs[9:]
    (send_outer, send_inner, keep_outer, keep_inner), pair_refs = packed[:4], packed[4:]
    me, odd_place = place_ref[0], place_ref[1] == 1
    terms, parts, loads, width = own_ref.shape
    copies = [
        [pltpu.make_async_copy(ref.at[:, c], staged.at[q, :, c], done.at[2 * c + q]) for q, ref in enumerate((own_ref, near_ref))]
        for c in range(parts)
    ]
    for pair in copies:
        for copy in pair:
            copy.start()
    out_copies = []
    cases = loads // 4
    lanes = rows.shape[3]
    for c in range(parts):
        for copy in copies[c]:
            copy.wait()
        for t in range(width // lanes):
            for q in range(2):
                piece = staged[q, :, c, :, t * lanes : (t + 1) * lanes].astype(jnp.float32)
                rows[c, t, q * terms * loads : (q + 1) * terms * loads] = piece.reshape(terms * loads, lanes)
            first, last = t * lanes, (t + 1) * lanes
            for m in range(cases):
                for outer, inner, x in ((send_outer, send_inner, 1 - (me >> 1)), (keep_outer, keep_inner, me >> 1)):
                    r = 4 * m + 2 * (me & 1) + x
                    both = rows[c, t, pl.ds(r, 2 * terms, stride=loads), :].astype(jnp.bfloat16).T
                    for ref, low, high, base in (
                        (outer, 0, TILE, 0),
                        (inner, TILE, width - TILE, 0),
                        (outer, width - TILE, width, TILE),
                    ):
                        low_row, high_row = max(low, first), min(high, last)
                        if low_row < high_row:
                            ref[m, c, base + low_row - low : base + high_row - low] = both[low_row - first : high_row - first]
        for m in range(cases):
            low, high = keep_outer[m, c, :TILE], keep_outer[m, c, TILE:]
            pair_refs[0][m, c] = jnp.where(odd_place, low, high)
            pair_refs[1][m, c] = jnp.where(odd_place, high, low)
        for i, (source, target) in enumerate(zip(packed, out_refs)):
            out_copies.append(pltpu.make_async_copy(source.at[:, c], target.at[:, c], done.at[2 * parts + 6 * c + i]))
            out_copies[-1].start()
    for copy in out_copies:
        copy.wait()


def pack(place, own, near):
    terms, parts, loads, width = own.shape
    cases = loads // 4
    shapes = [(cases, parts, 2 * TILE, 2 * terms), (cases, parts, width - 2 * TILE, 2 * terms)] * 2
    shapes += [(cases, parts, TILE, 2 * terms)] * 2
    return pl.pallas_call(
        pack_kernel,
        in_specs=[SMEM, ANY, ANY],
        out_specs=[HBM] * 6,
        scratch_shapes=[
            pltpu.VMEM((2, *near.shape), near.dtype),
            pltpu.VMEM((parts, width // 128, 2 * terms * loads, 128), jnp.float32),
            pltpu.SemaphoreType.DMA((8 * parts,)),
            *[pltpu.VMEM(shape, near.dtype) for shape in shapes],
        ],
        out_shape=[pltpu.HBM(shape, near.dtype) for shape in shapes],
        compiler_params=params(20),
        cost_estimate=SHORT,
    )(place, in_hbm(own), near)


def outer_kernel(place_ref, own_ref, far_ref, field_ref, even_ref, odd_ref, done):
    odd_place = place_ref[1] == 1
    cases, parts, _, half = own_ref.shape
    copies = [
        pltpu.make_async_copy(ref, field_ref.at[:, :, :, pl.ds(q * half, half)], done.at[q])
        for q, ref in ((1, far_ref), (0, own_ref))
    ]
    for copy in copies:
        copy.start()
    copies[0].wait()
    for m in range(cases):
        for c in range(parts):
            low, high = field_ref[m, c, :TILE, half:], field_ref[m, c, TILE:, half:]
            even_ref[m, c] = jnp.where(odd_place, low, high)
            odd_ref[m, c] = jnp.where(odd_place, high, low)
    copies[1].wait()


def gather_outer(place, own, far):
    cases, parts, height, half = own.shape
    edge = pltpu.VMEM((cases, parts, TILE, half), jnp.bfloat16)
    return pl.pallas_call(
        outer_kernel,
        in_specs=[SMEM, ANY, ANY],
        out_specs=[VMEM] * 3,
        scratch_shapes=[pltpu.SemaphoreType.DMA((2,))],
        out_shape=[pltpu.VMEM((cases, parts, height, 2 * half), jnp.bfloat16), edge, edge],
        compiler_params=params(4),
        cost_estimate=SHORT,
    )(place, in_hbm(own), far)


def swap(even, odd):
    count = lax.axis_size("space")
    even_pairs = [(i, i ^ 1) for i in range(count)]
    odd_pairs = [(i, ((i - 1) ^ 1) + 1) for i in range(1, count - 1)]
    return lax.ppermute(even, "space", even_pairs), lax.ppermute(odd, "space", odd_pairs)


def mix(fields, coupling_ref, slots, mixed):
    nkl, terms, _ = coupling_ref.shape
    for k in range(nkl):
        rows = slice(k * TILE, (k + 1) * TILE)
        for c, field in enumerate(fields):
            sums = jnp.dot(field, coupling_ref[k], preferred_element_type=jnp.float32).astype(jnp.bfloat16)
            for g, slot in enumerate(slots):
                mixed[slot, rows, c * terms : (c + 1) * terms] = sums[g * TILE : (g + 1) * TILE]


def mix_outer_kernel(field_ref, coupling_ref, mixed):
    def one_case(m, carry):
        mix([field_ref[m, c] for c in range(2)], coupling_ref, (0, mixed.shape[1] - 3), mixed.at[m])
        return carry

    lax.fori_loop(0, field_ref.shape[0], one_case, 0)


def mix_outer(field, coupling, blocks):
    cases, _, height, terms = field.shape
    nkl = coupling.shape[0]
    return pl.pallas_call(
        mix_outer_kernel,
        in_specs=[VMEM] * 2,
        out_specs=VMEM,
        out_shape=pltpu.VMEM((cases, blocks + 2, nkl * TILE, 2 * terms), jnp.bfloat16),
        compiler_params=params(4),
        cost_estimate=SHORT,
    )(*near_core(field, coupling))


def mix_inner_kernel(own_ref, far_ref, *refs):
    edge_refs = refs[: (len(refs) - 5) // 2]
    coupling_ref, _, mixed, *staged_refs, field_ref, done = refs[len(edge_refs) :]
    half = own_ref.shape[3]
    pairs = [
        (far_ref, field_ref.at[:, :, :, pl.ds(half, half)]),
        (own_ref, field_ref.at[:, :, :, pl.ds(0, half)]),
        *zip(edge_refs, staged_refs),
    ]
    copies = [pltpu.make_async_copy(source, target, done.at[i]) for i, (source, target) in enumerate(pairs)]
    for copy in copies:
        copy.start()
    for copy in copies[:2]:
        copy.wait()

    def one_case(m, carry):
        mix([field_ref[m, c] for c in range(2)], coupling_ref, range(1, mixed.shape[1] - 3), mixed.at[m])
        return carry

    lax.fori_loop(0, field_ref.shape[0], one_case, 0)
    for copy in copies[2:]:
        copy.wait()


def mix_inner(own, far, edges, coupling, mixed):
    cases, parts, height, half = own.shape
    nkl, terms, _ = coupling.shape
    count = len(edges)
    return pl.pallas_call(
        mix_inner_kernel,
        in_specs=[ANY] * (2 + count) + [VMEM] * 2,
        out_specs=[VMEM] * (1 + count),
        scratch_shapes=[
            pltpu.VMEM((cases, parts, height, terms), jnp.bfloat16),
            pltpu.SemaphoreType.DMA((2 + count,)),
        ],
        out_shape=[pltpu.VMEM(mixed.shape, mixed.dtype)] + [pltpu.VMEM(v.shape, v.dtype) for v in edges],
        input_output_aliases={3 + count: 0},
        compiler_params=params(8),
        cost_estimate=SHORT,
    )(in_hbm(own), far, *edges, *near_core(coupling, mixed))


def tiles_apply_kernel(m, quarters, place_ref, columns_ref, *refs):
    *edge_refs, coupling_ref, tiles_ref, _ = refs[:7]
    *out_refs, whole, flipped = refs[7:]
    terms = coupling_ref.shape[1]
    blocks, nnz = tiles_ref.shape[:2]
    half = terms // 2
    low, high = half * quarters[0], half * (quarters[-1] + 1)
    mixed = whole.at[m]

    def outer(c):
        even, odd, far_even, far_odd = (ref[m, c] for ref in edge_refs)
        return jnp.concatenate(
            [jnp.concatenate([even, far_even], axis=1), jnp.concatenate([odd, far_odd], axis=1)], axis=0
        )

    def slot_of(column):
        odd_place = place_ref[1]
        outside = jnp.where(column == 0, blocks + 1 - odd_place, blocks + odd_place)
        return jnp.where((column == 0) | (column == blocks + 1), outside, column - 1)

    if quarters[-1] == 1:
        mix([outer(c) for c in range(2)], coupling_ref, (blocks, blocks + 1), mixed)
    count = high - low
    for b in range(blocks):
        acc = None
        for s in range(nnz):
            slot = slot_of(columns_ref[b, s])
            field = jnp.concatenate([mixed[slot, :, c * terms + low : c * terms + high] for c in range(2)], axis=1)
            term = jnp.dot(tiles_ref[b, s], field, preferred_element_type=jnp.float32)
            acc = term if acc is None else acc + term
        rows = slice(b * TILE, (b + 1) * TILE)
        flipped[0, rows, :count] = (acc[:TILE, :count] - acc[TILE:, count:]).astype(jnp.bfloat16)
        flipped[1, rows, :count] = (acc[:TILE, count:] + acc[TILE:, :count]).astype(jnp.bfloat16)
    for c in range(2):
        part = flipped[c, :, :count].T
        for i, ref in enumerate(out_refs):
            ref[c] = part[i * half : (i + 1) * half]


def apply_tiles(m, place, columns, edges, coupling, tiles, mixed, quarters=(0, 1)):
    blocks, nnz, rows, depth = tiles.shape
    terms = coupling.shape[1]
    out = pltpu.VMEM((2, terms // 2, blocks * TILE), jnp.bfloat16)
    count = len(quarters)
    return pl.pallas_call(
        functools.partial(tiles_apply_kernel, m, quarters),
        in_specs=[SMEM] * 2 + [VMEM] * 7,
        out_specs=[VMEM] * (count + 1),
        scratch_shapes=[pltpu.VMEM((2, blocks * TILE, terms), jnp.bfloat16)],
        out_shape=[out] * count + [pltpu.VMEM(mixed.shape, mixed.dtype)],
        input_output_aliases={8: count},
        compiler_params=params(8),
        cost_estimate=SHORT,
    )(place, columns, *near_core(*edges, coupling, tiles, mixed))


def unpack_kernel(chunk, place_ref, *refs):
    me = place_ref[0]
    *piece_refs, out_ref, rows, done = refs
    parts, half, width = piece_refs[0].shape
    terms = half // 2
    loads = out_ref.shape[1] // 2
    lanes = rows.shape[2]
    copies = []
    for t in range(width // lanes):
        for position in range(loads):
            m, source = position // 4, me ^ (position % 4)
            r = 4 * m + 2 * (source & 1) + (source >> 1)
            first = terms * (position % 2)
            for c in range(parts):
                part = piece_refs[position][c, first : first + terms, t * lanes : (t + 1) * lanes]
                rows[t, pl.ds(c * loads + r, terms, stride=parts * loads), :] = part.astype(jnp.float32)
        source = rows.at[t].reshape(terms * parts, loads, lanes)
        target = out_ref.at[:, loads * chunk : loads * (chunk + 1), t * lanes : (t + 1) * lanes]
        copies.append(pltpu.make_async_copy(source, target, done.at[t]))
        copies[-1].start()
    for copy in copies:
        copy.wait()


def unpack(place, chunk, pieces, whole=None):
    parts, half, width = pieces[0].shape
    terms = half // 2
    loads = len(pieces)
    specs = [SMEM] + [VMEM] * loads
    aliases = {}
    if whole is not None:
        aliases = {len(pieces) + 1: 0}
        pieces = [*pieces, whole]
        specs = [*specs, ANY]

    def kernel(place_ref, *refs):
        refs = list(refs)
        if aliases:
            refs.pop(loads)
        unpack_kernel(chunk, place_ref, *refs)

    return pl.pallas_call(
        kernel,
        in_specs=specs,
        out_specs=ANY,
        scratch_shapes=[
            pltpu.VMEM((width // 128, terms * parts * loads, 128), jnp.float32),
            pltpu.SemaphoreType.DMA((width // 128,)),
        ],
        out_shape=jax.ShapeDtypeStruct((terms * parts, 2 * loads, width), jnp.float32),
        input_output_aliases=aliases,
        compiler_params=params(8),
        cost_estimate=SHORT,
    )(place, *pieces)


def after(value, *others):
    return lax.optimization_barrier((value, others))[0]


def body(load_vectors, stiff_tiles, tile_columns, chaos_index, chaos_value):
    count = lax.axis_size("chaos")
    blocks = stiff_tiles.shape[0]
    odd_place = lax.axis_index("space") % 2

    if count != 4:
        place = jnp.stack([jnp.zeros((), jnp.int32), odd_place])
        coupling = dense_coupling(place, chaos_index, chaos_value)
        tiles = wide_tiles(place, stiff_tiles)
        mine = lax.all_to_all(load_vectors, "chaos", split_axis=2, concat_axis=0, tiled=True)
        field = mine.transpose(2, 1, 3, 0)
        half = field.shape[3] // 2
        low, high = field[:, :, :TILE], field[:, :, -TILE:]
        swapped = swap(jnp.where(odd_place == 1, low, high), jnp.where(odd_place == 1, high, low))
        edges = [v[..., :half] for v in swapped] + [v[..., half:] for v in swapped]
        inner = field[:, :, TILE:-TILE]
        mixed = mix_outer(jnp.concatenate([low, high], axis=2), coupling, blocks)
        mixed = mix_inner(inner[..., :half], inner[..., half:], [], coupling, mixed)[0]
        cases = []
        for m in range(field.shape[0]):
            keep, send, mixed = apply_tiles(m, place, tile_columns, edges, coupling, tiles, mixed)
            cases.append(jnp.concatenate([keep, send], axis=1))
        result = jnp.stack(cases, axis=0)
        result = lax.all_to_all(result, "chaos", split_axis=2, concat_axis=0, tiled=True)
        return result.transpose(2, 1, 0, 3).astype(jnp.float32)

    place = jnp.stack([lax.axis_index("chaos"), odd_place])
    near = lambda v: lax.ppermute(v, "chaos", [(i, i ^ 1) for i in range(4)])
    across = lambda v: lax.ppermute(v, "chaos", [(i, i ^ 2) for i in range(4)])
    near_loads = near(load_vectors)
    tiles = wide_tiles(place, stiff_tiles)
    place = after(place, tiles)
    send_outer, send_inner, outer, inner, even, odd = pack(place, load_vectors, near_loads)
    far_outer = across(send_outer)
    own_edges = swap(even, odd)
    coupling = dense_coupling(after(place, even), chaos_index, chaos_value)
    far_inner = across(after(send_inner, coupling))
    field, even, odd = gather_outer(after(place, coupling, *own_edges), outer, far_outer)
    far_edges = swap(even, odd)
    mixed = mix_outer(field, coupling, blocks)
    mixed, *own_edges = mix_inner(inner, far_inner, own_edges, coupling, mixed)
    cases = field.shape[0]
    edges = [*own_edges, *far_edges]
    kept, near_kept, sent = [], [], []
    for m in range(cases):
        ready = after(place, *near_kept[m - 2 : m - 1], *sent[m - 3 : m - 2]) if m >= 2 else place
        given = ready, tile_columns, edges, coupling, tiles
        if m < cases - 1:
            keep, send, mixed = apply_tiles(m, *given, mixed)
        else:
            send, mixed = apply_tiles(m, *given, mixed, (1,))
            keep, mixed = apply_tiles(m, after(place, near_kept[m - 1], sent[m - 2]), *given[1:], mixed, (0,))
        kept.append(keep)
        near_kept.append(near(keep))
        sent.append(across(send))
    result = None
    for chunk in range(2):
        pieces = []
        for m in (2 * chunk, 2 * chunk + 1):
            back = after(sent[m], kept[-1] if result is None else result)
            pieces += [kept[m], near_kept[m], back, near(back)]
        result = unpack(after(place, sent[2]), chunk, pieces, result)
    return result.reshape(load_vectors.shape)


def solution(mesh):
    in_specs = (
        P("chaos", None, None, "space"),
        P("space", None, None, None, None, None),
        P("space", None),
        P(),
        P(),
    )
    out_specs = P("chaos", None, None, "space")
    return jax.shard_map(body, mesh=mesh, in_specs=in_specs, out_specs=out_specs, check_vma=False)
```

```python
import functools

import jax
import jax.numpy as jnp
from jax import lax
from jax.experimental import pallas as pl
from jax.experimental.pallas import tpu as pltpu
from jax.sharding import PartitionSpec as P

TILE = 96
VMEM = pl.BlockSpec(memory_space=pltpu.VMEM)
SMEM = pl.BlockSpec(memory_space=pltpu.SMEM)
ANY = pl.BlockSpec(memory_space=pl.ANY)
HBM = pl.BlockSpec(memory_space=pltpu.HBM)
SHORT = pl.CostEstimate(flops=1000, bytes_accessed=1000, transcendentals=0)


def near_core(*values):
    return [pltpu.with_memory_space_constraint(v, pltpu.VMEM) for v in values]


def in_hbm(value):
    return pltpu.with_memory_space_constraint(value, pltpu.HBM)


def params(mebibytes):
    return pltpu.CompilerParams(vmem_limit_bytes=mebibytes << 20)


def coupling_kernel(place_ref, index_hbm_ref, value_hbm_ref, out_ref, index_ref, value_ref, done):
    copies = [
        pltpu.make_async_copy(index_hbm_ref, index_ref, done.at[0]),
        pltpu.make_async_copy(value_hbm_ref, value_ref, done.at[1]),
    ]
    for copy in copies:
        copy.start()
    for copy in copies:
        copy.wait()
    me = place_ref[0]
    nkl, terms, _ = out_ref.shape
    share = terms // 4
    half = terms // 2

    def arrange(v):
        low, high = v[:, :half], v[:, half:]
        flip = (me >> 1) == 1
        first, second = jnp.where(flip, high, low), jnp.where(flip, low, high)
        shift = (me & 1) * share
        return jnp.concatenate([pltpu.roll(first, shift, 1), pltpu.roll(second, shift, 1)], axis=1)

    def one_term(k, carry):
        index = arrange(index_ref[k] ^ (me * share)).astype(jnp.float32).astype(jnp.bfloat16)
        value = arrange(value_ref[k].astype(jnp.float32)).astype(jnp.bfloat16)
        chunk = terms // 4
        for part in range(terms // chunk):
            j = lax.broadcasted_iota(jnp.int32, (chunk, terms), 0) + part * chunk
            j = j.astype(jnp.float32).astype(jnp.bfloat16)
            dense = jnp.zeros((chunk, terms), jnp.bfloat16)
            for n in range(index.shape[0]):
                dense = jnp.where(index[n : n + 1, :] == j, value[n : n + 1, :], dense)
            out_ref[k, part * chunk : (part + 1) * chunk, :] = dense
        return carry

    lax.fori_loop(0, nkl, one_term, 0)


def dense_coupling(place, chaos_index, chaos_value):
    nkl, terms, nzc = chaos_index.shape
    return pl.pallas_call(
        coupling_kernel,
        in_specs=[SMEM, ANY, ANY],
        out_specs=VMEM,
        scratch_shapes=[
            pltpu.VMEM((nkl, nzc, terms), chaos_index.dtype),
            pltpu.VMEM((nkl, nzc, terms), chaos_value.dtype),
            pltpu.SemaphoreType.DMA((2,)),
        ],
        out_shape=pltpu.VMEM((nkl, terms, terms), jnp.bfloat16),
        compiler_params=params(8),
        cost_estimate=SHORT,
    )(place, in_hbm(jnp.swapaxes(chaos_index, 1, 2)), in_hbm(jnp.swapaxes(chaos_value, 1, 2)))


def tiles_kernel(_, tiles_hbm_ref, out_ref, tiles_ref, done):
    blocks, nnz, nkl = tiles_ref.shape[:3]
    copies = [pltpu.make_async_copy(tiles_hbm_ref.at[b], tiles_ref.at[b], done.at[b]) for b in range(blocks)]
    for copy in copies:
        copy.start()
    for b in range(blocks):
        copies[b].wait()
        for s in range(nnz):
            for part in range(2):
                out_ref[b, s, part * TILE : (part + 1) * TILE, :] = jnp.concatenate(
                    [tiles_ref[b, s, k, part] for k in range(nkl)], axis=1
                )


def wide_tiles(place, stiff_tiles):
    blocks, nnz, nkl = stiff_tiles.shape[:3]
    return pl.pallas_call(
        tiles_kernel,
        in_specs=[SMEM, ANY],
        out_specs=VMEM,
        scratch_shapes=[pltpu.VMEM(stiff_tiles.shape, stiff_tiles.dtype), pltpu.SemaphoreType.DMA((blocks,))],
        out_shape=pltpu.VMEM((blocks, nnz, 2 * TILE, nkl * TILE), jnp.bfloat16),
        compiler_params=params(8),
        cost_estimate=SHORT,
    )(place, in_hbm(stiff_tiles))


def pack_kernel(place_ref, own_ref, near_ref, *refs):
    out_refs, (staged, rows, done), packed = refs[:6], refs[6:9], refs[9:]
    (send_outer, send_inner, keep_outer, keep_inner), pair_refs = packed[:4], packed[4:]
    me, odd_place = place_ref[0], place_ref[1] == 1
    terms, parts, loads, width = own_ref.shape
    copies = [
        [pltpu.make_async_copy(ref.at[:, c], staged.at[q, :, c], done.at[2 * c + q]) for q, ref in enumerate((own_ref, near_ref))]
        for c in range(parts)
    ]
    for pair in copies:
        for copy in pair:
            copy.start()
    out_copies = []
    cases = loads // 4
    lanes = rows.shape[3]
    for c in range(parts):
        for copy in copies[c]:
            copy.wait()
        for t in range(width // lanes):
            for q in range(2):
                piece = staged[q, :, c, :, t * lanes : (t + 1) * lanes].astype(jnp.float32)
                rows[c, t, q * terms * loads : (q + 1) * terms * loads] = piece.reshape(terms * loads, lanes)
            first, last = t * lanes, (t + 1) * lanes
            for m in range(cases):
                for outer, inner, x in ((send_outer, send_inner, 1 - (me >> 1)), (keep_outer, keep_inner, me >> 1)):
                    r = 4 * m + 2 * (me & 1) + x
                    both = rows[c, t, pl.ds(r, 2 * terms, stride=loads), :].astype(jnp.bfloat16).T
                    for ref, low, high, base in (
                        (outer, 0, TILE, 0),
                        (inner, TILE, width - TILE, 0),
                        (outer, width - TILE, width, TILE),
                    ):
                        low_row, high_row = max(low, first), min(high, last)
                        if low_row < high_row:
                            ref[m, c, base + low_row - low : base + high_row - low] = both[low_row - first : high_row - first]
        for m in range(cases):
            low, high = keep_outer[m, c, :TILE], keep_outer[m, c, TILE:]
            pair_refs[0][m, c] = jnp.where(odd_place, low, high)
            pair_refs[1][m, c] = jnp.where(odd_place, high, low)
        for i, (source, target) in enumerate(zip(packed, out_refs)):
            out_copies.append(pltpu.make_async_copy(source.at[:, c], target.at[:, c], done.at[2 * parts + 6 * c + i]))
            out_copies[-1].start()
    for copy in out_copies:
        copy.wait()


def pack(place, own, near):
    terms, parts, loads, width = own.shape
    cases = loads // 4
    shapes = [(cases, parts, 2 * TILE, 2 * terms), (cases, parts, width - 2 * TILE, 2 * terms)] * 2
    shapes += [(cases, parts, TILE, 2 * terms)] * 2
    return pl.pallas_call(
        pack_kernel,
        in_specs=[SMEM, ANY, ANY],
        out_specs=[HBM] * 6,
        scratch_shapes=[
            pltpu.VMEM((2, *near.shape), near.dtype),
            pltpu.VMEM((parts, width // 128, 2 * terms * loads, 128), jnp.float32),
            pltpu.SemaphoreType.DMA((8 * parts,)),
            *[pltpu.VMEM(shape, near.dtype) for shape in shapes],
        ],
        out_shape=[pltpu.HBM(shape, near.dtype) for shape in shapes],
        compiler_params=params(20),
        cost_estimate=SHORT,
    )(place, in_hbm(own), near)


def outer_kernel(place_ref, own_ref, far_ref, field_ref, even_ref, odd_ref, done):
    odd_place = place_ref[1] == 1
    cases, parts, _, half = own_ref.shape
    own_copy = pltpu.make_async_copy(own_ref, field_ref.at[:, :, :, pl.ds(0, half)], done.at[cases])
    copies = [
        pltpu.make_async_copy(far_ref.at[m], field_ref.at[m, :, :, pl.ds(half, half)], done.at[m]) for m in range(cases)
    ]
    for copy in [*copies, own_copy]:
        copy.start()
    for m in range(cases):
        copies[m].wait()
        for c in range(parts):
            low, high = field_ref[m, c, :TILE, half:], field_ref[m, c, TILE:, half:]
            even_ref[m, c] = jnp.where(odd_place, low, high)
            odd_ref[m, c] = jnp.where(odd_place, high, low)
    own_copy.wait()


def gather_outer(place, own, far):
    cases, parts, height, half = own.shape
    edge = pltpu.VMEM((cases, parts, TILE, half), jnp.bfloat16)
    return pl.pallas_call(
        outer_kernel,
        in_specs=[SMEM, ANY, ANY],
        out_specs=[VMEM] * 3,
        scratch_shapes=[pltpu.SemaphoreType.DMA((cases + 1,))],
        out_shape=[pltpu.VMEM((cases, parts, height, 2 * half), jnp.bfloat16), edge, edge],
        compiler_params=params(4),
        cost_estimate=SHORT,
    )(place, in_hbm(own), far)


def swap(even, odd):
    count = lax.axis_size("space")
    even_pairs = [(i, i ^ 1) for i in range(count)]
    odd_pairs = [(i, ((i - 1) ^ 1) + 1) for i in range(1, count - 1)]
    return lax.ppermute(even, "space", even_pairs), lax.ppermute(odd, "space", odd_pairs)


def mix(fields, coupling_ref, slots, mixed):
    nkl, terms, _ = coupling_ref.shape
    for k in range(nkl):
        rows = slice(k * TILE, (k + 1) * TILE)
        for c, field in enumerate(fields):
            sums = jnp.dot(field, coupling_ref[k], preferred_element_type=jnp.float32).astype(jnp.bfloat16)
            for g, slot in enumerate(slots):
                mixed[slot, rows, c * terms : (c + 1) * terms] = sums[g * TILE : (g + 1) * TILE]


def mix_outer_kernel(field_ref, coupling_ref, mixed):
    def one_case(m, carry):
        mix([field_ref[m, c] for c in range(2)], coupling_ref, (0, mixed.shape[1] - 3), mixed.at[m])
        return carry

    lax.fori_loop(0, field_ref.shape[0], one_case, 0)


def mix_outer(field, coupling, blocks):
    cases, _, height, terms = field.shape
    nkl = coupling.shape[0]
    return pl.pallas_call(
        mix_outer_kernel,
        in_specs=[VMEM] * 2,
        out_specs=VMEM,
        out_shape=pltpu.VMEM((cases, blocks + 2, nkl * TILE, 2 * terms), jnp.bfloat16),
        compiler_params=params(4),
        cost_estimate=SHORT,
    )(*near_core(field, coupling))


def mix_inner_kernel(own_ref, far_ref, *refs):
    edge_refs = refs[: (len(refs) - 5) // 2]
    coupling_ref, _, mixed, *staged_refs, field_ref, done = refs[len(edge_refs) :]
    half = own_ref.shape[3]
    cases = field_ref.shape[0]

    def parts_of(m):
        return [
            pltpu.make_async_copy(ref.at[m], field_ref.at[m, :, :, pl.ds(q * half, half)], done.at[2 * m + q])
            for q, ref in enumerate((own_ref, far_ref))
        ]

    for m in range(cases):
        for copy in parts_of(m):
            copy.start()
    copies = [
        pltpu.make_async_copy(source, target, done.at[2 * cases + i])
        for i, (source, target) in enumerate(zip(edge_refs, staged_refs))
    ]
    for copy in copies:
        copy.start()

    def one_case(m, carry):
        for copy in parts_of(m):
            copy.wait()
        mix([field_ref[m, c] for c in range(2)], coupling_ref, range(1, mixed.shape[1] - 3), mixed.at[m])
        return carry

    lax.fori_loop(0, field_ref.shape[0], one_case, 0)
    for copy in copies:
        copy.wait()


def mix_inner(own, far, edges, coupling, mixed):
    cases, parts, height, half = own.shape
    nkl, terms, _ = coupling.shape
    count = len(edges)
    return pl.pallas_call(
        mix_inner_kernel,
        in_specs=[ANY] * (2 + count) + [VMEM] * 2,
        out_specs=[VMEM] * (1 + count),
        scratch_shapes=[
            pltpu.VMEM((cases, parts, height, terms), jnp.bfloat16),
            pltpu.SemaphoreType.DMA((2 * cases + count,)),
        ],
        out_shape=[pltpu.VMEM(mixed.shape, mixed.dtype)] + [pltpu.VMEM(v.shape, v.dtype) for v in edges],
        input_output_aliases={3 + count: 0},
        compiler_params=params(8),
        cost_estimate=SHORT,
    )(in_hbm(own), far, *edges, *near_core(coupling, mixed))


def tiles_apply_kernel(m, quarters, place_ref, columns_ref, *refs):
    *edge_refs, coupling_ref, tiles_ref, _ = refs[:7]
    *out_refs, whole, flipped = refs[7:]
    terms = coupling_ref.shape[1]
    blocks, nnz = tiles_ref.shape[:2]
    half = terms // 2
    low, high = half * quarters[0], half * (quarters[-1] + 1)
    mixed = whole.at[m]

    def outer(c):
        even, odd, far_even, far_odd = (ref[m, c] for ref in edge_refs)
        return jnp.concatenate(
            [jnp.concatenate([even, far_even], axis=1), jnp.concatenate([odd, far_odd], axis=1)], axis=0
        )

    def slot_of(column):
        odd_place = place_ref[1]
        outside = jnp.where(column == 0, blocks + 1 - odd_place, blocks + odd_place)
        return jnp.where((column == 0) | (column == blocks + 1), outside, column - 1)

    if quarters[-1] == 1:
        mix([outer(c) for c in range(2)], coupling_ref, (blocks, blocks + 1), mixed)
    count = high - low
    for b in range(blocks):
        acc = None
        for s in range(nnz):
            slot = slot_of(columns_ref[b, s])
            field = jnp.concatenate([mixed[slot, :, c * terms + low : c * terms + high] for c in range(2)], axis=1)
            term = jnp.dot(tiles_ref[b, s], field, preferred_element_type=jnp.float32)
            acc = term if acc is None else acc + term
        rows = slice(b * TILE, (b + 1) * TILE)
        flipped[0, rows, :count] = (acc[:TILE, :count] - acc[TILE:, count:]).astype(jnp.bfloat16)
        flipped[1, rows, :count] = (acc[:TILE, count:] + acc[TILE:, :count]).astype(jnp.bfloat16)
    for c in range(2):
        part = flipped[c, :, :count].T
        for i, ref in enumerate(out_refs):
            ref[c] = part[i * half : (i + 1) * half]


def apply_tiles(m, place, columns, edges, coupling, tiles, mixed, quarters=(0, 1)):
    blocks, nnz, rows, depth = tiles.shape
    terms = coupling.shape[1]
    out = pltpu.VMEM((2, terms // 2, blocks * TILE), jnp.bfloat16)
    count = len(quarters)
    return pl.pallas_call(
        functools.partial(tiles_apply_kernel, m, quarters),
        in_specs=[SMEM] * 2 + [VMEM] * 7,
        out_specs=[VMEM] * (count + 1),
        scratch_shapes=[pltpu.VMEM((2, blocks * TILE, terms), jnp.bfloat16)],
        out_shape=[out] * count + [pltpu.VMEM(mixed.shape, mixed.dtype)],
        input_output_aliases={8: count},
        compiler_params=params(8),
        cost_estimate=SHORT,
    )(place, columns, *near_core(*edges, coupling, tiles, mixed))


def unpack_kernel(chunk, place_ref, *refs):
    me = place_ref[0]
    *piece_refs, out_ref, rows, done = refs
    parts, half, width = piece_refs[0].shape
    terms = half // 2
    loads = out_ref.shape[1] // 2
    lanes = rows.shape[2]
    copies = []
    for t in range(width // lanes):
        for position in range(loads):
            m, source = position // 4, me ^ (position % 4)
            r = 4 * m + 2 * (source & 1) + (source >> 1)
            first = terms * (position % 2)
            for c in range(parts):
                part = piece_refs[position][c, first : first + terms, t * lanes : (t + 1) * lanes]
                rows[t, pl.ds(c * loads + r, terms, stride=parts * loads), :] = part.astype(jnp.float32)
        source = rows.at[t].reshape(terms * parts, loads, lanes)
        target = out_ref.at[:, loads * chunk : loads * (chunk + 1), t * lanes : (t + 1) * lanes]
        copies.append(pltpu.make_async_copy(source, target, done.at[t]))
        copies[-1].start()
    for copy in copies:
        copy.wait()


def unpack(place, chunk, pieces, whole=None):
    parts, half, width = pieces[0].shape
    terms = half // 2
    loads = len(pieces)
    specs = [SMEM] + [VMEM] * loads
    aliases = {}
    if whole is not None:
        aliases = {len(pieces) + 1: 0}
        pieces = [*pieces, whole]
        specs = [*specs, ANY]

    def kernel(place_ref, *refs):
        refs = list(refs)
        if aliases:
            refs.pop(loads)
        unpack_kernel(chunk, place_ref, *refs)

    return pl.pallas_call(
        kernel,
        in_specs=specs,
        out_specs=ANY,
        scratch_shapes=[
            pltpu.VMEM((width // 128, terms * parts * loads, 128), jnp.float32),
            pltpu.SemaphoreType.DMA((width // 128,)),
        ],
        out_shape=jax.ShapeDtypeStruct((terms * parts, 2 * loads, width), jnp.float32),
        input_output_aliases=aliases,
        compiler_params=params(8),
        cost_estimate=SHORT,
    )(place, *pieces)


def after(value, *others):
    return lax.optimization_barrier((value, others))[0]


def body(load_vectors, stiff_tiles, tile_columns, chaos_index, chaos_value):
    count = lax.axis_size("chaos")
    blocks = stiff_tiles.shape[0]
    odd_place = lax.axis_index("space") % 2

    if count != 4:
        place = jnp.stack([jnp.zeros((), jnp.int32), odd_place])
        coupling = dense_coupling(place, chaos_index, chaos_value)
        tiles = wide_tiles(place, stiff_tiles)
        mine = lax.all_to_all(load_vectors, "chaos", split_axis=2, concat_axis=0, tiled=True)
        field = mine.transpose(2, 1, 3, 0)
        half = field.shape[3] // 2
        low, high = field[:, :, :TILE], field[:, :, -TILE:]
        swapped = swap(jnp.where(odd_place == 1, low, high), jnp.where(odd_place == 1, high, low))
        edges = [v[..., :half] for v in swapped] + [v[..., half:] for v in swapped]
        inner = field[:, :, TILE:-TILE]
        mixed = mix_outer(jnp.concatenate([low, high], axis=2), coupling, blocks)
        mixed = mix_inner(inner[..., :half], inner[..., half:], [], coupling, mixed)[0]
        cases = []
        for m in range(field.shape[0]):
            keep, send, mixed = apply_tiles(m, place, tile_columns, edges, coupling, tiles, mixed)
            cases.append(jnp.concatenate([keep, send], axis=1))
        result = jnp.stack(cases, axis=0)
        result = lax.all_to_all(result, "chaos", split_axis=2, concat_axis=0, tiled=True)
        return result.transpose(2, 1, 0, 3).astype(jnp.float32)

    place = jnp.stack([lax.axis_index("chaos"), odd_place])
    near = lambda v: lax.ppermute(v, "chaos", [(i, i ^ 1) for i in range(4)])
    across = lambda v: lax.ppermute(v, "chaos", [(i, i ^ 2) for i in range(4)])
    near_loads = near(load_vectors)
    tiles = wide_tiles(place, stiff_tiles)
    place = after(place, tiles)
    send_outer, send_inner, outer, inner, even, odd = pack(place, load_vectors, near_loads)
    far_outer = across(send_outer)
    own_edges = swap(even, odd)
    coupling = dense_coupling(after(place, even), chaos_index, chaos_value)
    far_inner = across(after(send_inner, coupling))
    field, even, odd = gather_outer(after(place, coupling, *own_edges), outer, far_outer)
    far_edges = swap(even, odd)
    mixed = mix_outer(field, coupling, blocks)
    mixed, *own_edges = mix_inner(inner, far_inner, own_edges, coupling, mixed)
    cases = field.shape[0]
    edges = [*own_edges, *far_edges]
    kept, near_kept, sent = [], [], []
    for m in range(cases):
        ready = after(place, *near_kept[m - 2 : m - 1], *sent[m - 3 : m - 2]) if m >= 2 else place
        given = ready, tile_columns, edges, coupling, tiles
        if m < cases - 1:
            keep, send, mixed = apply_tiles(m, *given, mixed)
        else:
            send, mixed = apply_tiles(m, *given, mixed, (1,))
            keep, mixed = apply_tiles(m, after(place, near_kept[m - 1], sent[m - 2]), *given[1:], mixed, (0,))
        kept.append(keep)
        near_kept.append(near(keep))
        sent.append(across(send))
    result = None
    for chunk in range(2):
        pieces = []
        for m in (2 * chunk, 2 * chunk + 1):
            back = after(sent[m], kept[-1] if result is None else result)
            pieces += [kept[m], near_kept[m], back, near(back)]
        result = unpack(after(place, sent[2]), chunk, pieces, result)
    return result.reshape(load_vectors.shape)


def solution(mesh):
    in_specs = (
        P("chaos", None, None, "space"),
        P("space", None, None, None, None, None),
        P("space", None),
        P(),
        P(),
    )
    out_specs = P("chaos", None, None, "space")
    return jax.shard_map(body, mesh=mesh, in_specs=in_specs, out_specs=out_specs, check_vma=False)
```
